32 devices in a mesh: ord: 16 (over z, y, x), rhs: 2 (over core).
Axes of the slice: x: 2, y: 2, z: 4, core: 2. Of those that a mesh axis runs over, the one named last changes fastest.
Arguments:
- rhs_blocks: float32 [128, 640, 128], P('ord', None, 'rhs'), may hold values from -6 to 6
- rhs_border: float32 [512, 128], P(None, 'rhs'), may hold values from -6 to 6
- start_blocks: float32 [128, 640, 128], P('ord', None, 'rhs'), may hold values from -3 to 3
- start_border: float32 [512, 128], P(None, 'rhs'), may hold values from -3 to 3
- diag_blocks: bfloat16 [128, 640, 640], P('ord'), may hold values from -1 to 9
- block_inverses: bfloat16 [128, 640, 640], P('ord'), may hold values from -6 to 6
- couplings: bfloat16 [128, 640, 640], P('ord'), may hold values from -0.125 to 0.125
- border_couplings: bfloat16 [128, 640, 512], P('ord'), may hold values from -0.01953125 to 0.01953125
- border_block: bfloat16 [512, 512], replicated, may hold values from -1 to 9
- schur_inverse: float32 [512, 512], replicated, may hold values from -6 to 6
- row_counts: int32 [128], P('ord'), may hold values from 1 to 640, as said below
Outputs:
- solution_blocks: float32 [128, 640, 128], P('ord', None, 'rhs')
- solution_border: float32 [512, 128], P(None, 'rhs')
The draws below stay inside these ranges and needn't reach their ends.
Inputs may be any that keep to these rules, and one draw needn't show every extreme that they name: row_counts[m] is the number of live rows of order block m; block 0 has exactly 640 rows and the counts fall with the order to about a third of 640.
All inputs are finite; a program needn't handle non-finite values.
Results may differ from the reference program's by a relative error of at most 0.0035.
Values may be sent and summed in bfloat16 or wider, within the bound.
A program may use at most 128 MiB of HBM per device.

```python
import math
import jax
import jax.numpy as jnp
from jax import lax

BR = 640
NB = 512
RHS = 128
ITERS = 3
MB = 128


def dominant_pair(base_key, mat_order, lead_shape):
    scale_key = jax.random.fold_in(base_key, 11)
    noise_key = jax.random.fold_in(base_key, 12)
    low_end, high_end = (1.0, 4.0)
    vec_shape = tuple(lead_shape) + (mat_order,)
    diagonal = jnp.exp(jax.random.uniform(scale_key, vec_shape, jnp.float32, math.log(low_end), math.log(high_end)))
    coupled = jnp.clip(jax.random.normal(noise_key, tuple(lead_shape) + (mat_order, mat_order), jnp.float32), -4.0, 4.0)
    coupled = (coupled + jnp.swapaxes(coupled, -1, -2)) * (0.5 / math.sqrt(2.0 * mat_order))
    identity = jnp.eye(mat_order, dtype=jnp.float32)
    matrix = coupled + diagonal[..., :, None] * identity
    reciprocal = 1.0 / diagonal
    inverse = reciprocal[..., :, None] * identity - reciprocal[..., :, None] * coupled * reciprocal[..., None, :]
    return (matrix, inverse)


def draw_diag_blocks(key, part):
    matrix, inverse = dominant_pair(jax.random.fold_in(key, 101), BR, (MB,))
    return matrix.astype(jnp.bfloat16)


def draw_block_inverses(key, part):
    matrix, inverse = dominant_pair(jax.random.fold_in(key, 101), BR, (MB,))
    return inverse.astype(jnp.bfloat16)


def draw_border_block(key, part):
    matrix, inverse = dominant_pair(jax.random.fold_in(key, 202), NB, ())
    return matrix.astype(jnp.bfloat16)


def draw_schur_inverse(key, part):
    matrix, inverse = dominant_pair(jax.random.fold_in(key, 202), NB, ())
    return inverse.astype(jnp.float32)


def draw_row_counts(key, part):
    blocks = jnp.arange(MB, dtype=jnp.int32)
    falling = blocks * (2 * BR // 3) // MB
    jitter = jax.random.randint(jax.random.fold_in(key, 303), (MB,), 0, BR // 16 + 1, dtype=jnp.int32)
    jitter = jnp.where(blocks == 0, 0, jitter)
    return (BR - falling - jitter).astype(jnp.int32)


def block_levels(key, shape, split, low, largest):
    level = 1.0
    for axis_at, parts in split:
        heights = jax.random.uniform(jax.random.fold_in(jax.random.fold_in(key, 6), axis_at), (parts,), jnp.float32, low / len(split), largest / len(split))
        level = level * jnp.repeat(jnp.exp(heights), shape[axis_at] // parts).reshape((-1,) + (1,) * (len(shape) - 1 - axis_at))
    return level


def scatter_about(rng, extent, spread, reach, shards=(), kind=jnp.bfloat16):
    drawn = spread * jax.random.normal(rng, extent, jnp.float32)
    if shards:
        drawn = drawn * block_levels(rng, extent, shards, -0.22, 0.18)
    return jnp.clip(drawn, -reach, reach).astype(kind)


def setup_inputs(seed: int = 0) -> dict:
    streams_of = jax.random.split(jax.random.key(seed), 12)
    rhs_blocks = scatter_about(streams_of[0], (MB, BR, RHS), 1.0, 6.0, ((0, 16), (2, 2)), jnp.float32)
    rhs_border = scatter_about(streams_of[1], (NB, RHS), 1.0, 6.0, ((1, 2),), jnp.float32)
    start_blocks = scatter_about(streams_of[2], (MB, BR, RHS), 0.5, 3.0, ((0, 16), (2, 2)), jnp.float32)
    start_border = scatter_about(streams_of[3], (NB, RHS), 0.5, 3.0, ((1, 2),), jnp.float32)
    diag_blocks = draw_diag_blocks(jax.random.fold_in(streams_of[11], 71), 0)
    block_inverses = draw_block_inverses(jax.random.fold_in(streams_of[11], 71), 0)
    couplings = scatter_about(streams_of[6], (MB, BR, BR), (4 * BR) ** -0.5, 0.125, ((0, 16),))
    border_couplings = scatter_about(streams_of[7], (MB, BR, NB), (BR * MB) ** -0.5, 0.01953125, ((0, 16),))
    border_block = draw_border_block(jax.random.fold_in(streams_of[11], 71), 0)
    schur_inverse = draw_schur_inverse(jax.random.fold_in(streams_of[11], 71), 0)
    row_counts = draw_row_counts(jax.random.fold_in(streams_of[11], 71), 0)
    return dict(rhs_blocks=rhs_blocks, rhs_border=rhs_border, start_blocks=start_blocks, start_border=start_border, diag_blocks=diag_blocks, block_inverses=block_inverses, couplings=couplings, border_couplings=border_couplings, border_block=border_block, schur_inverse=schur_inverse, row_counts=row_counts)


def widen(array):
    return array.astype(jnp.float32)


def rounded(array):
    return lax.optimization_barrier(array.astype(jnp.bfloat16)).astype(jnp.float32)


def batched(matrices, vectors):
    return jnp.einsum('mij,mjc->mic', matrices, vectors, precision=lax.Precision.HIGHEST)


def reference(rhs_blocks, rhs_border, start_blocks, start_border, diag_blocks, block_inverses, couplings, border_couplings, border_block, schur_inverse, row_counts):
    live_rows = (jnp.arange(BR, dtype=jnp.int32)[None, :] < row_counts[:, None]).astype(jnp.float32)[:, :, None]
    wide_diag = widen(diag_blocks)
    wide_inverse = widen(block_inverses)
    wide_coupling = widen(couplings)
    wide_border = widen(border_couplings)

    def operate(state, state_border):
        wide_state = rounded(state)
        narrow_border = state_border.astype(jnp.bfloat16)
        following = jnp.concatenate([wide_state[1:], jnp.zeros_like(wide_state[:1])], 0)
        ahead = batched(wide_coupling, following)
        transposed = jnp.einsum('mji,mjc->mic', wide_coupling, wide_state, precision=lax.Precision.HIGHEST)
        behind = jnp.concatenate([jnp.zeros_like(transposed[:1]), transposed[:-1]], 0)
        from_border = jnp.einsum('mib,bc->mic', wide_border, widen(narrow_border), precision=lax.Precision.HIGHEST)
        applied = live_rows * (batched(wide_diag, wide_state) + ahead + behind + from_border)
        gathered = jnp.einsum('mib,mic->bc', wide_border, wide_state, precision=lax.Precision.HIGHEST)
        applied_border = jnp.dot(border_block, narrow_border, preferred_element_type=jnp.float32) + gathered
        return applied, applied_border

    def precondition(residual, resid_border):
        blockwise = live_rows * batched(wide_inverse, rounded(residual))
        border_sum = jnp.einsum('mib,mic->bc', wide_border, rounded(blockwise), precision=lax.Precision.HIGHEST)
        update_border = jnp.dot(schur_inverse, resid_border - border_sum, precision=lax.Precision.HIGHEST)
        lifted = rounded(jnp.einsum('mib,bc->mic', wide_border, rounded(update_border), precision=lax.Precision.HIGHEST))
        update = blockwise - live_rows * batched(wide_inverse, lifted)
        return update, update_border

    solution = live_rows * start_blocks
    solution_border = start_border
    applied, applied_border = operate(solution, solution_border)
    residual = live_rows * rhs_blocks - applied
    resid_border = rhs_border - applied_border
    for iteration in range(ITERS):
        update, update_border = precondition(residual, resid_border)
        applied, applied_border = operate(update, update_border)
        numerator = jnp.sum(residual * applied) + jnp.sum(resid_border * applied_border)
        denominator = jnp.sum(applied * applied) + jnp.sum(applied_border * applied_border)
        step_size = numerator / (denominator + 1e-6)
        solution = solution + step_size * update
        solution_border = solution_border + step_size * update_border
        residual = residual - step_size * applied
        resid_border = resid_border - step_size * applied_border
    return solution, solution_border
```

```python
import functools

import jax
import jax.numpy as jnp
from jax import lax
from jax.experimental import pallas as pl
from jax.experimental.pallas import tpu as pltpu
from jax.sharding import PartitionSpec as P

ITERS = 3
MESH = pl.DeviceIdType.MESH


def shifted(value, axis, steps):
    count = lax.axis_size(axis)
    leading, last = (max(0, -steps), min(count, count - steps))
    return lax.ppermute(value, axis, [(source, source + steps) for source in range(leading, last)])


def batched(matrices, vectors):
    return jnp.einsum("sij,sjc->sic", matrices, vectors, preferred_element_type=jnp.float32)


def total_kernel(
    count,
    part_ref,
    own_ref,
    resid_ref,
    scalars_ref,
    sum_ref,
    total_ref,
    landing,
    message,
    gathered,
    mine,
    theirs,
    send_a,
    recv_a,
    send_b,
    recv_b,
    send_c,
    recv_c,
):
    me = lax.axis_index("ord")
    core = lax.axis_index("rhs")
    rows = part_ref.shape[0] // count
    border_columns = own_ref.shape[1]
    other_core = 1 - core

    def peer(step):
        return lax.rem(me + step, count)

    def source(step):
        return lax.rem(me + count - step, count)

    barrier = pltpu.get_barrier_semaphore()

    def greet(step, carry):
        pl.semaphore_signal(barrier, inc=1, device_id=(peer(step), core), device_id_type=MESH)
        return carry

    lax.fori_loop(1, count, greet, 0)
    pl.semaphore_signal(barrier, inc=1, device_id=(me, other_core), device_id_type=MESH)
    pl.semaphore_wait(barrier, count)

    def rows_of(device):
        return pl.ds(pl.multiple_of(device * rows, rows), rows)

    def scatter(step):
        return pltpu.make_async_remote_copy(
            src_ref=part_ref.at[rows_of(peer(step))],
            dst_ref=landing.at[step],
            send_sem=send_a.at[step],
            recv_sem=recv_a.at[step],
            device_id=(peer(step), core),
            device_id_type=MESH,
        )

    def scatter_start(step, carry):
        scatter(step).start()
        return carry

    def scatter_wait(step, reduced):
        scatter(step).wait_recv()
        return reduced + landing[step]

    lax.fori_loop(1, count, scatter_start, 0)
    reduced = lax.fori_loop(1, count, scatter_wait, part_ref[rows_of(me)])

    applied = own_ref[rows_of(me)] + reduced[:, :border_columns]
    numerator = jnp.sum(resid_ref[rows_of(me)] * applied)
    denominator = jnp.sum(applied * applied)
    tile_row = lax.broadcasted_iota(jnp.int32, (8, part_ref.shape[1]), 0)
    border_scalars = jnp.where(
        tile_row == 0, numerator, jnp.where(tile_row == 1, denominator, 0.0)
    )
    message[:rows] = reduced
    message[rows:] = scalars_ref[...] + border_scalars

    def gather(step):
        return pltpu.make_async_remote_copy(
            src_ref=message,
            dst_ref=gathered.at[me],
            send_sem=send_b.at[step],
            recv_sem=recv_b.at[step],
            device_id=(peer(step), core),
            device_id_type=MESH,
        )

    def gather_landed(step):
        return pltpu.make_async_remote_copy(
            src_ref=message,
            dst_ref=gathered.at[source(step)],
            send_sem=send_b.at[step],
            recv_sem=recv_b.at[step],
            device_id=(peer(step), core),
            device_id_type=MESH,
        )

    def gather_start(step, carry):
        gather(step).start()
        return carry

    def gather_wait(step, carry):
        gather_landed(step).wait_recv()
        return carry

    lax.fori_loop(1, count, gather_start, 0)
    gathered[me] = message[...]
    lax.fori_loop(1, count, gather_wait, 0)

    def add_scalars(device, so_far):
        return so_far + gathered[device, rows:, :]

    mine[...] = lax.fori_loop(1, count, add_scalars, gathered[0, rows:, :])
    pair = pltpu.make_async_remote_copy(
        src_ref=mine,
        dst_ref=theirs,
        send_sem=send_c,
        recv_sem=recv_c,
        device_id=(me, other_core),
        device_id_type=MESH,
    )
    pair.start()
    for device in range(count):
        sum_ref[device * rows : (device + 1) * rows, :] = gathered[device, :rows, :]
    pair.wait_recv()
    total_ref[...] = mine[...] + theirs[...]
    pair.wait_send()

    def drain(step, carry):
        scatter(step).wait_send()
        gather(step).wait_send()
        return carry

    lax.fori_loop(1, count, drain, 0)


def border_total(part, own, resid, scalars, collective_id):
    count = lax.axis_size("ord")
    border_rows, columns = part.shape
    rows = border_rows // count
    numerator, denominator = scalars
    tile_row = lax.broadcasted_iota(jnp.int32, (8, columns), 0)
    tile = jnp.where(tile_row == 0, numerator, jnp.where(tile_row == 1, denominator, 0.0))
    tile = tile.astype(jnp.float32)
    whole = pl.BlockSpec(memory_space=pltpu.VMEM)
    summed, totals = pl.pallas_call(
        functools.partial(total_kernel, count),
        out_shape=(
            jax.ShapeDtypeStruct((border_rows, columns), jnp.float32),
            jax.ShapeDtypeStruct((8, columns), jnp.float32),
        ),
        in_specs=[whole] * 4,
        out_specs=(whole, whole),
        scratch_shapes=[
            pltpu.VMEM((count, rows, columns), jnp.float32),
            pltpu.VMEM((rows + 8, columns), jnp.float32),
            pltpu.VMEM((count, rows + 8, columns), jnp.float32),
            pltpu.VMEM((8, columns), jnp.float32),
            pltpu.VMEM((8, columns), jnp.float32),
            pltpu.SemaphoreType.DMA((count,)),
            pltpu.SemaphoreType.DMA((count,)),
            pltpu.SemaphoreType.DMA((count,)),
            pltpu.SemaphoreType.DMA((count,)),
            pltpu.SemaphoreType.DMA,
            pltpu.SemaphoreType.DMA,
        ],
        compiler_params=pltpu.CompilerParams(
            collective_id=collective_id, has_side_effects=True
        ),
        name="border_total",
    )(part, own, resid, tile)
    return (summed, totals[0, 0], totals[1, 0])


def shards(
    rhs_blocks,
    rhs_border,
    start_blocks,
    start_border,
    diag_blocks,
    block_inverses,
    couplings,
    border_couplings,
    border_block,
    schur_inverse,
    row_counts,
):
    slot_count = rhs_blocks.shape[0]
    row_total = rhs_blocks.shape[1]
    columns = rhs_blocks.shape[2]
    live_rows = (
        lax.broadcasted_iota(jnp.int32, (slot_count, row_total), 1) < row_counts[:, None]
    ).astype(jnp.float32)[:, :, None]

    def to_border(state):
        return jnp.einsum(
            "sib,sic->bc", border_couplings, state, preferred_element_type=jnp.float32
        )

    def operate(narrow, narrow_border):
        transposed = jnp.einsum(
            "sji,sjc->sic", couplings, narrow, preferred_element_type=jnp.float32
        )
        lower = shifted(transposed[slot_count - 1 :].astype(jnp.bfloat16), "ord", 1).astype(
            jnp.float32
        )
        upper = shifted(narrow[:1], "ord", -1)
        ahead = batched(couplings, jnp.concatenate([narrow[1:], upper], 0))
        behind = jnp.concatenate([lower, transposed[:-1]], 0)
        from_border = jnp.einsum(
            "sib,bc->sic", border_couplings, narrow_border, preferred_element_type=jnp.float32
        )
        return live_rows * (batched(diag_blocks, narrow) + ahead + behind + from_border)

    def border_product(narrow_border):
        return jnp.dot(border_block, narrow_border, preferred_element_type=jnp.float32)

    solution = live_rows * start_blocks
    solution_border = start_border
    narrow = solution.astype(jnp.bfloat16)
    narrow_border = solution_border.astype(jnp.bfloat16)
    own_border = border_product(narrow_border)
    residual = live_rows * rhs_blocks - operate(narrow, narrow_border)
    blockwise = live_rows * batched(block_inverses, residual.astype(jnp.bfloat16))
    part = jnp.concatenate([to_border(narrow), to_border(blockwise.astype(jnp.bfloat16))], 1)
    summed, unused_num, unused_den = border_total(part, own_border, rhs_border, (0.0, 0.0), 1)
    resid_border = rhs_border - (own_border + summed[:, :columns])
    total_sum = summed[:, columns:]
    for iteration in range(ITERS):
        update_border = jnp.dot(
            schur_inverse, resid_border - total_sum, precision=lax.Precision.HIGHEST
        )
        narrow_border = update_border.astype(jnp.bfloat16)
        lifted = jnp.einsum(
            "sib,bc->sic",
            border_couplings,
            narrow_border,
            preferred_element_type=jnp.float32,
        ).astype(jnp.bfloat16)
        update = blockwise - live_rows * batched(block_inverses, lifted)
        narrow = update.astype(jnp.bfloat16)
        applied = operate(narrow, narrow_border)
        own_border = border_product(narrow_border)
        scalars = (jnp.sum(residual * applied), jnp.sum(applied * applied))
        more = iteration < ITERS - 1
        if more:
            change = live_rows * batched(block_inverses, applied.astype(jnp.bfloat16))
            part = jnp.concatenate(
                [to_border(narrow), to_border(change.astype(jnp.bfloat16))], 1
            )
        else:
            part = to_border(narrow)
        summed, numerator, denominator = border_total(
            part, own_border, resid_border, scalars, 1 if more else 2
        )
        step_size = numerator / (denominator + 1e-06)
        solution = solution + step_size * update
        solution_border = solution_border + step_size * update_border
        if more:
            applied_border = own_border + summed[:, :columns]
            residual = residual - step_size * applied
            resid_border = resid_border - step_size * applied_border
            blockwise = live_rows * batched(block_inverses, residual.astype(jnp.bfloat16))
            total_sum = total_sum - step_size * summed[:, columns:]
    return (solution, solution_border)


def solution(mesh):
    return jax.shard_map(
        shards,
        mesh=mesh,
        in_specs=(
            P("ord", None, "rhs"),
            P(None, "rhs"),
            P("ord", None, "rhs"),
            P(None, "rhs"),
            P("ord", None, None),
            P("ord", None, None),
            P("ord", None, None),
            P("ord", None, None),
            P(),
            P(),
            P("ord"),
        ),
        out_specs=(P("ord", None, "rhs"), P(None, "rhs")),
        check_vma=False,
    )
```

```python
import functools

import jax
import jax.numpy as jnp
from jax import lax
from jax.experimental import pallas as pl
from jax.experimental.pallas import tpu as pltpu
from jax.sharding import PartitionSpec as P

ITERS = 3
MESH = pl.DeviceIdType.MESH
F32 = jnp.float32
BF16 = jnp.bfloat16


def mm(left, right):
    return jnp.dot(left, right, preferred_element_type=F32)


def kernel(
    count,
    rhs_hbm,
    start_hbm,
    diag_hbm,
    inverse_hbm,
    coupling_hbm,
    border_hbm,
    rhs_border_ref,
    start_border_ref,
    corner_ref,
    schur_ref,
    counts_ref,
    out_ref,
    out_border_ref,
    diag,
    inverse,
    coupling,
    coupling_t,
    border,
    border_t,
    rhs_own,
    rhs_land,
    start_own,
    start_land,
    rhs_border_land,
    start_border_land,
    sol,
    resid,
    update,
    applied,
    narrow,
    upper,
    lower_send,
    lower,
    resid_b,
    sol_b,
    update_b,
    own_b,
    schur_sum,
    part,
    pair_land,
    reduced,
    landing,
    message,
    gathered,
    total,
    out_send,
    out_land,
    load_sem,
    swap_send,
    swap_recv,
    halo_send,
    halo_recv,
    pair_send,
    pair_recv,
    send_b,
    recv_b,
    send_c,
    recv_c,
):
    me = lax.axis_index("ord")
    core = lax.axis_index("rhs")
    other = 1 - core
    first = core == 0
    slots, row_total, half = rhs_own.shape
    columns = 2 * half
    border_rows = resid_b.shape[0]
    rows = border_rows // count
    own_slots = pl.ds(core * slots, slots)
    other_slots = pl.ds(other * slots, slots)

    loads = [
        pltpu.make_async_copy(source.at[own_slots], target, load_sem.at[at])
        for at, (source, target) in enumerate(
            (
                (start_hbm, start_own),
                (coupling_hbm, coupling),
                (border_hbm, border),
                (diag_hbm, diag),
                (rhs_hbm, rhs_own),
                (inverse_hbm, inverse),
            )
        )
    ]
    for load in loads:
        load.start()

    def peer(step):
        return lax.rem(me + step, count)

    def source(step):
        return lax.rem(me + count - step, count)

    sibling = (me, other)
    beyond = (lax.rem(me + count + jnp.where(first, -1, 1), count), other)
    following = (jnp.where(first, me, lax.rem(me + 1, count)), other)
    preceding = (jnp.where(first, lax.rem(me + count - 1, count), me), other)

    barrier = pltpu.get_barrier_semaphore()

    def greet(step, carry):
        pl.semaphore_signal(barrier, inc=1, device_id=(peer(step), core), device_id_type=MESH)
        return carry

    lax.fori_loop(1, count, greet, 0)
    pl.semaphore_signal(barrier, inc=1, device_id=sibling, device_id_type=MESH)
    pl.semaphore_signal(barrier, inc=1, device_id=beyond, device_id_type=MESH)
    pl.semaphore_wait(barrier, count + 1)

    def remote(source_ref, target_ref, send_sem, recv_sem, device):
        return pltpu.make_async_remote_copy(
            src_ref=source_ref,
            dst_ref=target_ref,
            send_sem=send_sem,
            recv_sem=recv_sem,
            device_id=device,
            device_id_type=MESH,
        )

    swaps = [
        remote(source_ref, target, swap_send.at[at], swap_recv.at[at], sibling)
        for at, (source_ref, target) in enumerate(
            (
                (start_hbm.at[other_slots], start_land),
                (start_border_ref, start_border_land),
                (rhs_hbm.at[other_slots], rhs_land),
                (rhs_border_ref, rhs_border_land),
            )
        )
    ]
    for swap in swaps:
        swap.start()

    def joined(own, theirs):
        return jnp.concatenate(
            [jnp.where(first, own, theirs), jnp.where(first, theirs, own)], 1
        )

    def live(slot, value):
        at_row = lax.broadcasted_iota(jnp.int32, value.shape, 0)
        return jnp.where(at_row < counts_ref[core * slots + slot], value, 0.0)

    def each_slot(body):
        def step(slot, carry):
            body(slot)
            return carry

        lax.fori_loop(0, slots, step, 0)

    def folded(value):
        return jnp.sum(value.reshape(row_total // 8, 8, columns), axis=0)

    def operate(border_narrow):
        last = slots - 1
        lower_send[...] = mm(coupling_t[last], narrow[last]).astype(BF16)
        down = remote(lower_send, lower, halo_send.at[0], halo_recv.at[0], following)
        up = remote(narrow.at[0], upper, halo_send.at[1], halo_recv.at[1], preceding)
        down.start()
        up.start()
        own_b[...] = mm(corner_ref[...], border_narrow)

        def local(slot):
            return mm(diag[slot], narrow[slot]) + mm(border[slot], border_narrow)

        def behind(slot):
            return mm(coupling_t[slot - 1], narrow[slot - 1])

        def inner(slot, carry):
            applied[slot] = local(slot) + mm(coupling[slot], narrow[slot + 1]) + behind(slot)
            return carry

        lax.fori_loop(1, last, inner, 0)
        top = local(0) + mm(coupling[0], narrow[1])
        applied[last] = local(last) + behind(last)
        down.wait_recv()
        is_first = jnp.logical_and(me == 0, first)
        applied[0] = top + jnp.where(is_first, 0.0, lower[...].astype(F32))
        up.wait_recv()
        is_last = jnp.logical_and(me == count - 1, core == 1)
        ahead = jnp.where(is_last, 0.0, upper[...].astype(F32)).astype(BF16)
        applied[last] = applied[last] + mm(coupling[last], ahead)
        down.wait_send()
        up.wait_send()

    def rows_of(device):
        return pl.ds(pl.multiple_of(device * rows, rows), rows)

    def sum_border(numerators, denominators):
        swap = remote(
            part.at[other], pair_land, pair_send.at[0], pair_recv.at[0], sibling
        )
        swap.start()
        swap.wait_recv()
        reduced[...] = part[core] + pair_land[...]

        def scatter(step):
            return remote(
                reduced.at[rows_of(peer(step))],
                landing.at[step],
                send_b.at[step],
                recv_b.at[step],
                (peer(step), core),
            )

        def scatter_start(step, carry):
            scatter(step).start()
            return carry

        def scatter_wait(step, so_far):
            scatter(step).wait_recv()
            return so_far + landing[step]

        lax.fori_loop(1, count, scatter_start, 0)
        mine = lax.fori_loop(1, count, scatter_wait, reduced[rows_of(me)])
        border_part = jnp.where(first, own_b[rows_of(me)] + mine, 0.0)
        against = resid_b[rows_of(me)] * border_part
        squares = border_part * border_part
        message[:rows] = mine
        message[rows : rows + 8] = numerators + jnp.sum(
            against.reshape(rows // 8, 8, columns), axis=0
        )
        message[rows + 8 :] = denominators + jnp.sum(
            squares.reshape(rows // 8, 8, columns), axis=0
        )

        def gather(step, slot):
            return remote(
                message,
                gathered.at[slot],
                send_c.at[step],
                recv_c.at[step],
                (peer(step), core),
            )

        def gather_start(step, carry):
            gather(step, me).start()
            return carry

        def gather_wait(step, carry):
            gather(step, source(step)).wait_recv()
            return carry

        lax.fori_loop(1, count, gather_start, 0)
        gathered[me] = message[...]
        lax.fori_loop(1, count, gather_wait, 0)

        def place(device, tiles):
            total[core, rows_of(device)] = gathered[device, :rows, :]
            return tiles + gathered[device, rows:, :]

        tiles = lax.fori_loop(0, count, place, jnp.zeros((16, columns), F32))
        total[core, border_rows:] = tiles
        back = remote(
            total.at[core], total.at[core], pair_send.at[1], pair_recv.at[1], sibling
        )
        back.start()
        landed = remote(
            total.at[other], total.at[other], pair_send.at[1], pair_recv.at[1], sibling
        )
        landed.wait_recv()
        back.wait_send()
        swap.wait_send()

        def drain(step, carry):
            scatter(step).wait_send()
            gather(step, me).wait_send()
            return carry

        lax.fori_loop(1, count, drain, 0)
        both = total[0, border_rows:] + total[1, border_rows:]
        return (jnp.sum(both[:8]), jnp.sum(both[8:]))

    zero_tile = jnp.zeros((8, columns), F32)

    loads[0].wait()
    swaps[0].wait_recv()

    def begin(slot):
        value = live(slot, joined(start_own[slot], start_land[slot]))
        sol[slot] = value
        narrow[slot] = value.astype(BF16)

    each_slot(begin)
    loads[1].wait()

    def turn_coupling(slot):
        coupling_t[slot] = coupling[slot].T

    each_slot(turn_coupling)
    loads[2].wait()

    def turn_border(slot):
        border_t[slot] = border[slot].T

    each_slot(turn_border)
    swaps[1].wait_recv()
    sol_b[...] = joined(start_border_ref[...], start_border_land[...])
    loads[3].wait()
    operate(sol_b[...].astype(BF16))
    loads[4].wait()
    loads[5].wait()
    swaps[2].wait_recv()
    swaps[3].wait_recv()
    part[...] = jnp.zeros_like(part)

    def to_border(slot, blockwise):
        pair = jnp.concatenate([narrow[slot], blockwise.astype(BF16)], 1)
        sums = mm(border_t[slot], pair)
        part[0] = part[0] + sums[:, :columns]
        part[1] = part[1] + sums[:, columns:]

    def first_residual(slot):
        value = live(slot, joined(rhs_own[slot], rhs_land[slot]) - applied[slot])
        resid[slot] = value
        to_border(slot, live(slot, mm(inverse[slot], value.astype(BF16))))

    each_slot(first_residual)
    resid_b[...] = joined(rhs_border_ref[...], rhs_border_land[...])
    sum_border(zero_tile, zero_tile)
    resid_b[...] = resid_b[...] - (own_b[...] + total[0, :border_rows])
    schur_sum[...] = total[1, :border_rows]

    step_size = None
    for iteration in range(ITERS):
        more = iteration < ITERS - 1
        update_b[...] = jnp.dot(
            schur_ref[...],
            resid_b[...] - schur_sum[...],
            precision=lax.Precision.HIGHEST,
            preferred_element_type=F32,
        )
        border_narrow = update_b[...].astype(BF16)

        def precondition(slot, step_size=step_size, border_narrow=border_narrow):
            if step_size is not None:
                sol[slot] = sol[slot] + step_size * update[slot]
                resid[slot] = resid[slot] - step_size * applied[slot]
            lifted = mm(border[slot], border_narrow).astype(BF16)
            both = mm(
                inverse[slot], jnp.concatenate([resid[slot].astype(BF16), lifted], 1)
            )
            value = live(slot, both[:, :columns] - both[:, columns:])
            update[slot] = value
            narrow[slot] = value.astype(BF16)

        each_slot(precondition)
        operate(border_narrow)
        part[...] = jnp.zeros_like(part)

        def products(slot, carry, more=more):
            numerators, denominators = carry
            value = live(slot, applied[slot])
            applied[slot] = value
            if more:
                to_border(slot, live(slot, mm(inverse[slot], value.astype(BF16))))
            else:
                part[0] = part[0] + mm(border_t[slot], narrow[slot])
            return (
                numerators + folded(resid[slot] * value),
                denominators + folded(value * value),
            )

        tiles = lax.fori_loop(0, slots, products, (zero_tile, zero_tile))
        numerator, denominator = sum_border(*tiles)
        step_size = numerator / (denominator + 1e-06)
        sol_b[...] = sol_b[...] + step_size * update_b[...]
        if more:
            applied_b = own_b[...] + total[0, :border_rows]
            resid_b[...] = resid_b[...] - step_size * applied_b
            schur_sum[...] = schur_sum[...] - step_size * total[1, :border_rows]

    def finish(slot):
        value = sol[slot] + step_size * update[slot]
        left, right = (value[:, :half], value[:, half:])
        out_ref[core * slots + slot] = jnp.where(first, left, right)
        out_send[slot] = jnp.where(first, right, left)

    each_slot(finish)
    share = remote(out_send, out_land, swap_send.at[4], swap_recv.at[4], sibling)
    share.start()
    out_border_ref[...] = jnp.where(first, sol_b[:, :half], sol_b[:, half:])
    for swap in swaps:
        swap.wait_send()
    share.wait_recv()

    def place_out(slot):
        out_ref[other * slots + slot] = out_land[slot]

    each_slot(place_out)
    share.wait_send()


def shards(
    rhs_blocks,
    rhs_border,
    start_blocks,
    start_border,
    diag_blocks,
    block_inverses,
    couplings,
    border_couplings,
    border_block,
    schur_inverse,
    row_counts,
):
    count = lax.axis_size("ord")
    slots = rhs_blocks.shape[0] // 2
    row_total, half = rhs_blocks.shape[1:]
    columns = 2 * half
    border_rows = rhs_border.shape[0]
    rows = border_rows // count
    vmem = pl.BlockSpec(memory_space=pltpu.VMEM)
    anywhere = pl.BlockSpec(memory_space=pl.ANY)
    square = pltpu.VMEM((slots, row_total, row_total), BF16)
    halves = pltpu.VMEM((slots, row_total, half), F32)
    border_half = pltpu.VMEM((border_rows, half), F32)
    state = pltpu.VMEM((slots, row_total, columns), F32)
    edge = pltpu.VMEM((row_total, columns), BF16)
    border_state = pltpu.VMEM((border_rows, columns), F32)
    sems = pltpu.SemaphoreType.DMA
    return pl.pallas_call(
        functools.partial(kernel, count),
        out_shape=(
            jax.ShapeDtypeStruct(rhs_blocks.shape, F32),
            jax.ShapeDtypeStruct(rhs_border.shape, F32),
        ),
        in_specs=[anywhere] * 6 + [vmem] * 4 + [pl.BlockSpec(memory_space=pltpu.SMEM)],
        out_specs=(vmem, vmem),
        scratch_shapes=[
            square,
            square,
            square,
            square,
            pltpu.VMEM((slots, row_total, border_rows), BF16),
            pltpu.VMEM((slots, border_rows, row_total), BF16),
            halves,
            halves,
            halves,
            halves,
            border_half,
            border_half,
            state,
            state,
            state,
            state,
            pltpu.VMEM((slots, row_total, columns), BF16),
            edge,
            edge,
            edge,
            border_state,
            border_state,
            border_state,
            border_state,
            border_state,
            pltpu.VMEM((2, border_rows, columns), F32),
            border_state,
            border_state,
            pltpu.VMEM((count, rows, columns), F32),
            pltpu.VMEM((rows + 16, columns), F32),
            pltpu.VMEM((count, rows + 16, columns), F32),
            pltpu.VMEM((2, border_rows + 16, columns), F32),
            halves,
            halves,
            sems((6,)),
            sems((5,)),
            sems((5,)),
            sems((2,)),
            sems((2,)),
            sems((2,)),
            sems((2,)),
            sems((count,)),
            sems((count,)),
            sems((count,)),
            sems((count,)),
        ],
        compiler_params=pltpu.CompilerParams(
            collective_id=0, has_side_effects=True, vmem_limit_bytes=58 * 2**20
        ),
        name="minimal_residual",
    )(
        rhs_blocks,
        start_blocks,
        diag_blocks,
        block_inverses,
        couplings,
        border_couplings,
        rhs_border,
        start_border,
        border_block,
        schur_inverse,
        row_counts,
    )


def solution(mesh):
    return jax.shard_map(
        shards,
        mesh=mesh,
        in_specs=(
            P("ord", None, "rhs"),
            P(None, "rhs"),
            P("ord", None, "rhs"),
            P(None, "rhs"),
            P("ord", None, None),
            P("ord", None, None),
            P("ord", None, None),
            P("ord", None, None),
            P(),
            P(),
            P("ord"),
        ),
        out_specs=(P("ord", None, "rhs"), P(None, "rhs")),
        check_vma=False,
    )
```

```python
import functools

import jax
import jax.numpy as jnp
from jax import lax
from jax.experimental import pallas as pl
from jax.experimental.pallas import tpu as pltpu
from jax.sharding import PartitionSpec as P

ITERS = 3
MESH = pl.DeviceIdType.MESH
F32 = jnp.float32
BF16 = jnp.bfloat16


def mm(left, right):
    return jnp.dot(left, right, preferred_element_type=F32)


def kernel(
    count,
    rhs_hbm,
    start_hbm,
    diag_hbm,
    inverse_hbm,
    coupling_hbm,
    border_hbm,
    rhs_border_ref,
    start_border_ref,
    corner_ref,
    schur_ref,
    counts_ref,
    out_ref,
    out_border_ref,
    diag,
    inverse,
    coupling,
    coupling_t,
    border,
    border_t,
    rhs_own,
    rhs_land,
    start_own,
    start_land,
    rhs_border_land,
    start_border_land,
    sol,
    resid,
    update,
    applied,
    narrow,
    upper,
    lower_send,
    lower,
    resid_b,
    sol_b,
    update_b,
    own_b,
    schur_sum,
    part,
    pair_land,
    reduced,
    landing,
    message,
    gathered,
    last_tiles,
    total,
    out_send,
    out_land,
    load_sem,
    swap_send,
    swap_recv,
    halo_send,
    halo_recv,
    pair_send,
    pair_recv,
    send_b,
    recv_b,
    send_c,
    recv_c,
    recv_last,
):
    me = lax.axis_index("ord")
    core = lax.axis_index("rhs")
    other = 1 - core
    first = core == 0
    slots, half, row_total = rhs_own.shape
    columns = 2 * half
    border_rows = resid_b.shape[0]
    rows = border_rows // count
    own_slots = pl.ds(core * slots, slots)
    other_slots = pl.ds(other * slots, slots)

    loads = [
        pltpu.make_async_copy(source.at[own_slots], target, load_sem.at[at])
        for at, (source, target) in enumerate(
            (
                (start_hbm, start_own),
                (coupling_hbm, coupling),
                (border_hbm, border),
                (diag_hbm, diag),
                (rhs_hbm, rhs_own),
                (inverse_hbm, inverse),
            )
        )
    ]
    for load in loads:
        load.start()

    def peer(step):
        ahead = me + step
        return jnp.where(ahead >= count, ahead - count, ahead)

    def source(step):
        behind = me - step
        return jnp.where(behind < 0, behind + count, behind)

    sibling = (me, other)
    beyond = (lax.rem(me + count + jnp.where(first, -1, 1), count), other)
    following = (jnp.where(first, me, lax.rem(me + 1, count)), other)
    preceding = (jnp.where(first, lax.rem(me + count - 1, count), me), other)

    barrier = pltpu.get_barrier_semaphore()

    def greet(step, carry):
        pl.semaphore_signal(barrier, inc=1, device_id=(peer(step), core), device_id_type=MESH)
        return carry

    lax.fori_loop(1, count, greet, 0)
    pl.semaphore_signal(barrier, inc=1, device_id=sibling, device_id_type=MESH)
    pl.semaphore_signal(barrier, inc=1, device_id=beyond, device_id_type=MESH)
    pl.semaphore_wait(barrier, count + 1)

    def remote(source_ref, target_ref, send_sem, recv_sem, device):
        return pltpu.make_async_remote_copy(
            src_ref=source_ref,
            dst_ref=target_ref,
            send_sem=send_sem,
            recv_sem=recv_sem,
            device_id=device,
            device_id_type=MESH,
        )

    swaps = [
        remote(source_ref, target, swap_send.at[at], swap_recv.at[at], sibling)
        for at, (source_ref, target) in enumerate(
            (
                (start_hbm.at[other_slots], start_land),
                (start_border_ref, start_border_land),
                (rhs_hbm.at[other_slots], rhs_land),
                (rhs_border_ref, rhs_border_land),
            )
        )
    ]
    for swap in swaps:
        swap.start()

    def joined(own, theirs):
        return jnp.concatenate(
            [jnp.where(first, own, theirs), jnp.where(first, theirs, own)], 0
        ).T

    def live(slot, value):
        at_row = lax.broadcasted_iota(jnp.int32, value.shape, 0)
        return jnp.where(at_row < counts_ref[core * slots + slot], value, 0.0)

    def each_slot(body):
        def step(slot, carry):
            body(slot)
            return carry

        lax.fori_loop(0, slots, step, 0)

    def folded(value):
        return jnp.sum(value.reshape(row_total // 8, 8, columns), axis=0)

    def operate(border_narrow):
        last = slots - 1
        lower_send[...] = mm(coupling_t[last], narrow[last]).astype(BF16)
        down = remote(lower_send, lower, halo_send.at[0], halo_recv.at[0], following)
        up = remote(narrow.at[0], upper, halo_send.at[1], halo_recv.at[1], preceding)
        down.start()
        up.start()
        own_b[...] = mm(corner_ref[...], border_narrow)

        def local(slot):
            return mm(diag[slot], narrow[slot]) + mm(border[slot], border_narrow)

        def behind(slot):
            return mm(coupling_t[slot - 1], narrow[slot - 1])

        def inner(slot, carry):
            applied[slot] = local(slot) + mm(coupling[slot], narrow[slot + 1]) + behind(slot)
            return carry

        lax.fori_loop(1, last, inner, 0)
        top = local(0) + mm(coupling[0], narrow[1])
        applied[last] = local(last) + behind(last)
        down.wait_recv()
        is_first = jnp.logical_and(me == 0, first)
        applied[0] = top + jnp.where(is_first, 0.0, lower[...].astype(F32))
        up.wait_recv()
        is_last = jnp.logical_and(me == count - 1, core == 1)
        ahead = jnp.where(is_last, 0.0, upper[...].astype(F32)).astype(BF16)
        applied[last] = applied[last] + mm(coupling[last], ahead)
        down.wait_send()
        up.wait_send()

    def rows_of(device):
        return pl.ds(pl.multiple_of(device * rows, rows), rows)

    def sum_border(numerators, denominators, final=False):
        swap = remote(
            part.at[other], pair_land, pair_send.at[0], pair_recv.at[0], sibling
        )
        swap.start()
        swap.wait_recv()
        reduced[...] = part[core] + pair_land[...]

        def scatter(step):
            return remote(
                reduced.at[rows_of(peer(step))],
                landing.at[step],
                send_b.at[step],
                recv_b.at[step],
                (peer(step), core),
            )

        def scatter_start(step, carry):
            scatter(step).start()
            return carry

        def scatter_wait(step, so_far):
            scatter(step).wait_recv()
            return so_far + landing[step]

        def scatter_drain(step, carry):
            scatter(step).wait_send()
            return carry

        def reduce_rows():
            lax.fori_loop(1, count, scatter_start, 0)
            message[:rows] = lax.fori_loop(1, count, scatter_wait, reduced[rows_of(me)])

        if final:
            pl.when(first)(reduce_rows)
        else:
            reduce_rows()
        mine = message[:rows]
        border_part = jnp.where(first, own_b[rows_of(me)] + mine, 0.0)
        against = resid_b[rows_of(me)] * border_part
        squares = border_part * border_part
        numerators = numerators + jnp.sum(against.reshape(rows // 8, 8, columns), axis=0)
        denominators = denominators + jnp.sum(squares.reshape(rows // 8, 8, columns), axis=0)
        tile_row = lax.broadcasted_iota(jnp.int32, (8, columns), 0)
        message[rows:] = jnp.where(
            tile_row == 0,
            jnp.sum(numerators, axis=0, keepdims=True),
            jnp.where(tile_row == 1, jnp.sum(denominators, axis=0, keepdims=True), 0.0),
        )

        def gather(step, slot):
            return remote(
                message.at[pl.ds(rows, 8)] if final else message,
                last_tiles.at[slot] if final else gathered.at[slot],
                send_c.at[step],
                recv_last.at[step] if final else recv_c.at[step],
                (peer(step), core),
            )

        def gather_start(step, carry):
            gather(step, me).start()
            return carry

        def gather_wait(step, carry):
            gather(step, source(step)).wait_recv()
            return carry

        lax.fori_loop(1, count, gather_start, 0)
        if final:
            last_tiles[me] = message[rows:]
        else:
            gathered[me] = message[...]
        lax.fori_loop(1, count, gather_wait, 0)

        def place(device, tiles):
            if final:
                return tiles + last_tiles[device]
            total[core, rows_of(device)] = gathered[device, :rows, :]
            return tiles + gathered[device, rows:, :]

        tiles = lax.fori_loop(0, count, place, jnp.zeros((8, columns), F32))
        total[core, border_rows:] = tiles

        def half_total(owner):
            ref = total.at[owner, pl.ds(border_rows, 8)] if final else total.at[owner]
            return remote(ref, ref, pair_send.at[1], pair_recv.at[1], sibling)

        back = half_total(core)
        back.start()
        landed = half_total(other)
        landed.wait_recv()
        back.wait_send()
        swap.wait_send()

        def drain(step, carry):
            gather(step, me).wait_send()
            return carry

        def drain_rows():
            lax.fori_loop(1, count, scatter_drain, 0)

        if final:
            pl.when(first)(drain_rows)
        else:
            drain_rows()
        lax.fori_loop(1, count, drain, 0)
        both = total[0, border_rows:] + total[1, border_rows:]
        return (jnp.sum(both[0:1]), jnp.sum(both[1:2]))

    zero_tile = jnp.zeros((8, columns), F32)

    loads[0].wait()
    swaps[0].wait_recv()

    def begin(slot):
        value = live(slot, joined(start_own[slot], start_land[slot]))
        sol[slot] = value
        narrow[slot] = value.astype(BF16)

    each_slot(begin)
    loads[1].wait()

    def turn_coupling(slot):
        coupling_t[slot] = coupling[slot].T

    each_slot(turn_coupling)
    loads[2].wait()

    def turn_border(slot):
        border_t[slot] = border[slot].T

    each_slot(turn_border)
    swaps[1].wait_recv()
    sol_b[...] = joined(start_border_ref[...], start_border_land[...])
    loads[3].wait()
    operate(sol_b[...].astype(BF16))
    loads[4].wait()
    loads[5].wait()
    swaps[2].wait_recv()
    swaps[3].wait_recv()
    part[...] = jnp.zeros_like(part)

    def to_border(slot, blockwise):
        pair = jnp.concatenate([narrow[slot], blockwise.astype(BF16)], 1)
        sums = mm(border_t[slot], pair)
        part[0] = part[0] + sums[:, :columns]
        part[1] = part[1] + sums[:, columns:]

    def first_residual(slot):
        value = live(slot, joined(rhs_own[slot], rhs_land[slot]) - applied[slot])
        resid[slot] = value
        to_border(slot, live(slot, mm(inverse[slot], value.astype(BF16))))

    each_slot(first_residual)
    resid_b[...] = joined(rhs_border_ref[...], rhs_border_land[...])
    sum_border(zero_tile, zero_tile)
    resid_b[...] = resid_b[...] - (own_b[...] + total[0, :border_rows])
    schur_sum[...] = total[1, :border_rows]

    step_size = None
    for iteration in range(ITERS):
        more = iteration < ITERS - 1
        update_b[...] = jnp.dot(
            schur_ref[...],
            resid_b[...] - schur_sum[...],
            precision=lax.Precision.HIGHEST,
            preferred_element_type=F32,
        )
        border_narrow = update_b[...].astype(BF16)

        def precondition(slot, step_size=step_size, border_narrow=border_narrow):
            if step_size is not None:
                sol[slot] = sol[slot] + step_size * update[slot]
                resid[slot] = resid[slot] - step_size * applied[slot]
            lifted = mm(border[slot], border_narrow).astype(BF16)
            both = mm(
                inverse[slot], jnp.concatenate([resid[slot].astype(BF16), lifted], 1)
            )
            value = live(slot, both[:, :columns] - both[:, columns:])
            update[slot] = value
            narrow[slot] = value.astype(BF16)

        each_slot(precondition)
        operate(border_narrow)
        part[...] = jnp.zeros_like(part)

        def products(slot, carry, more=more):
            numerators, denominators = carry
            value = live(slot, applied[slot])
            applied[slot] = value
            if more:
                to_border(slot, live(slot, mm(inverse[slot], value.astype(BF16))))
            else:
                part[0] = part[0] + mm(border_t[slot], narrow[slot])
            return (
                numerators + folded(resid[slot] * value),
                denominators + folded(value * value),
            )

        tiles = lax.fori_loop(0, slots, products, (zero_tile, zero_tile))
        numerator, denominator = sum_border(*tiles, final=not more)
        step_size = numerator / (denominator + 1e-06)
        sol_b[...] = sol_b[...] + step_size * update_b[...]
        if more:
            applied_b = own_b[...] + total[0, :border_rows]
            resid_b[...] = resid_b[...] - step_size * applied_b
            schur_sum[...] = schur_sum[...] - step_size * total[1, :border_rows]

    def finish(slot):
        value = sol[slot] + step_size * update[slot]
        turned = value.T
        left, right = (turned[:half], turned[half:])
        out_ref[core * slots + slot] = jnp.where(first, left, right)
        out_send[slot] = jnp.where(first, right, left)

    each_slot(finish)
    share = remote(out_send, out_land, swap_send.at[4], swap_recv.at[4], sibling)
    share.start()
    turned_b = sol_b[...].T
    out_border_ref[...] = jnp.where(first, turned_b[:half], turned_b[half:])
    for swap in swaps:
        swap.wait_send()
    share.wait_recv()

    def place_out(slot):
        out_ref[other * slots + slot] = out_land[slot]

    each_slot(place_out)
    share.wait_send()


def shards(
    rhs_blocks,
    rhs_border,
    start_blocks,
    start_border,
    diag_blocks,
    block_inverses,
    couplings,
    border_couplings,
    border_block,
    schur_inverse,
    row_counts,
):
    count = lax.axis_size("ord")
    slots = rhs_blocks.shape[0] // 2
    row_total, half = rhs_blocks.shape[1:]
    columns = 2 * half
    border_rows = rhs_border.shape[0]
    rows = border_rows // count
    vmem = pl.BlockSpec(memory_space=pltpu.VMEM)
    anywhere = pl.BlockSpec(memory_space=pl.ANY)
    square = pltpu.VMEM((slots, row_total, row_total), BF16)
    halves = pltpu.VMEM((slots, half, row_total), F32)
    border_half = pltpu.VMEM((half, border_rows), F32)
    state = pltpu.VMEM((slots, row_total, columns), F32)
    edge = pltpu.VMEM((row_total, columns), BF16)
    border_state = pltpu.VMEM((border_rows, columns), F32)
    sems = pltpu.SemaphoreType.DMA
    turned_blocks, turned_border = pl.pallas_call(
        functools.partial(kernel, count),
        out_shape=(
            jax.ShapeDtypeStruct((2 * slots, half, row_total), F32),
            jax.ShapeDtypeStruct((half, border_rows), F32),
        ),
        in_specs=[anywhere] * 6 + [vmem] * 4 + [pl.BlockSpec(memory_space=pltpu.SMEM)],
        out_specs=(vmem, vmem),
        scratch_shapes=[
            square,
            square,
            square,
            square,
            pltpu.VMEM((slots, row_total, border_rows), BF16),
            pltpu.VMEM((slots, border_rows, row_total), BF16),
            halves,
            halves,
            halves,
            halves,
            border_half,
            border_half,
            state,
            state,
            state,
            state,
            pltpu.VMEM((slots, row_total, columns), BF16),
            edge,
            edge,
            edge,
            border_state,
            border_state,
            border_state,
            border_state,
            border_state,
            pltpu.VMEM((2, border_rows, columns), F32),
            border_state,
            border_state,
            pltpu.VMEM((count, rows, columns), F32),
            pltpu.VMEM((rows + 8, columns), F32),
            pltpu.VMEM((count, rows + 8, columns), F32),
            pltpu.VMEM((count, 8, columns), F32),
            pltpu.VMEM((2, border_rows + 8, columns), F32),
            halves,
            halves,
            sems((6,)),
            sems((5,)),
            sems((5,)),
            sems((2,)),
            sems((2,)),
            sems((2,)),
            sems((2,)),
            sems((count,)),
            sems((count,)),
            sems((count,)),
            sems((count,)),
            sems((count,)),
        ],
        compiler_params=pltpu.CompilerParams(
            collective_id=0, has_side_effects=True, vmem_limit_bytes=58 * 2**20
        ),
        name="minimal_residual",
    )(
        jnp.swapaxes(rhs_blocks, 1, 2),
        jnp.swapaxes(start_blocks, 1, 2),
        diag_blocks,
        block_inverses,
        couplings,
        border_couplings,
        rhs_border.T,
        start_border.T,
        border_block,
        schur_inverse,
        row_counts,
    )
    return (jnp.swapaxes(turned_blocks, 1, 2), turned_border.T)


def solution(mesh):
    return jax.shard_map(
        shards,
        mesh=mesh,
        in_specs=(
            P("ord", None, "rhs"),
            P(None, "rhs"),
            P("ord", None, "rhs"),
            P(None, "rhs"),
            P("ord", None, None),
            P("ord", None, None),
            P("ord", None, None),
            P("ord", None, None),
            P(),
            P(),
            P("ord"),
        ),
        out_specs=(P("ord", None, "rhs"), P(None, "rhs")),
        check_vma=False,
    )
```

```python
import functools

import jax
import jax.numpy as jnp
from jax import lax
from jax.experimental import pallas as pl
from jax.experimental.pallas import tpu as pltpu
from jax.sharding import PartitionSpec as P

ITERS = 3
MESH = pl.DeviceIdType.MESH
F32 = jnp.float32
BF16 = jnp.bfloat16


def mm(left, right):
    return jnp.dot(left, right, preferred_element_type=F32)


def kernel(
    count,
    rhs_hbm,
    start_hbm,
    diag_hbm,
    inverse_hbm,
    coupling_hbm,
    border_hbm,
    rhs_border_ref,
    start_border_ref,
    corner_ref,
    schur_ref,
    counts_ref,
    out_ref,
    out_border_ref,
    diag,
    inverse,
    coupling,
    coupling_t,
    border,
    border_t,
    rhs_own,
    rhs_land,
    start_own,
    start_land,
    rhs_border_land,
    start_border_land,
    sol,
    resid,
    update,
    applied,
    narrow,
    upper,
    lower_send,
    lower,
    resid_b,
    sol_b,
    update_b,
    own_b,
    schur_sum,
    part,
    pair_land,
    reduced,
    landing,
    message,
    gathered,
    last_tiles,
    total,
    out_send,
    out_land,
    load_sem,
    swap_send,
    swap_recv,
    halo_send,
    halo_recv,
    pair_send,
    pair_recv,
    send_b,
    recv_b,
    send_c,
    recv_c,
    recv_last,
):
    me = lax.axis_index("ord")
    core = lax.axis_index("rhs")
    other = 1 - core
    first = core == 0
    slots, half, row_total = rhs_own.shape
    columns = 2 * half
    border_rows = resid_b.shape[0]
    rows = border_rows // count
    own_slots = pl.ds(core * slots, slots)
    other_slots = pl.ds(other * slots, slots)

    loads = [
        pltpu.make_async_copy(source.at[own_slots], target, load_sem.at[at])
        for at, (source, target) in enumerate(
            (
                (start_hbm, start_own),
                (coupling_hbm, coupling),
                (border_hbm, border),
                (diag_hbm, diag),
                (rhs_hbm, rhs_own),
                (inverse_hbm, inverse),
            )
        )
    ]
    for load in loads:
        load.start()

    def peer(step):
        ahead = me + step
        return jnp.where(ahead >= count, ahead - count, ahead)

    def source(step):
        behind = me - step
        return jnp.where(behind < 0, behind + count, behind)

    sibling = (me, other)
    beyond = (lax.rem(me + count + jnp.where(first, -1, 1), count), other)
    following = (jnp.where(first, me, lax.rem(me + 1, count)), other)
    preceding = (jnp.where(first, lax.rem(me + count - 1, count), me), other)

    barrier = pltpu.get_barrier_semaphore()

    def greet(step, carry):
        pl.semaphore_signal(barrier, inc=1, device_id=(peer(step), core), device_id_type=MESH)
        return carry

    lax.fori_loop(1, count, greet, 0)
    pl.semaphore_signal(barrier, inc=1, device_id=sibling, device_id_type=MESH)
    pl.semaphore_signal(barrier, inc=1, device_id=beyond, device_id_type=MESH)
    pl.semaphore_wait(barrier, count + 1)

    def remote(source_ref, target_ref, send_sem, recv_sem, device):
        return pltpu.make_async_remote_copy(
            src_ref=source_ref,
            dst_ref=target_ref,
            send_sem=send_sem,
            recv_sem=recv_sem,
            device_id=device,
            device_id_type=MESH,
        )

    swaps = [
        remote(source_ref, target, swap_send.at[at], swap_recv.at[at], sibling)
        for at, (source_ref, target) in enumerate(
            (
                (start_hbm.at[other_slots], start_land),
                (start_border_ref, start_border_land),
                (rhs_hbm.at[other_slots], rhs_land),
                (rhs_border_ref, rhs_border_land),
            )
        )
    ]
    for swap in swaps:
        swap.start()

    def joined(own, theirs):
        return jnp.concatenate(
            [jnp.where(first, own, theirs), jnp.where(first, theirs, own)], 0
        ).T

    def live(slot, value):
        at_row = lax.broadcasted_iota(jnp.int32, value.shape, 0)
        return jnp.where(at_row < counts_ref[core * slots + slot], value, 0.0)

    def each_slot(body):
        def step(slot, carry):
            body(slot)
            return carry

        lax.fori_loop(0, slots, step, 0)

    def folded(value):
        return jnp.sum(value.reshape(row_total // 8, 8, columns), axis=0)

    def operate(border_narrow):
        last = slots - 1
        lower_send[...] = mm(coupling_t[last], narrow[last]).astype(BF16)
        down = remote(lower_send, lower, halo_send.at[0], halo_recv.at[0], following)
        up = remote(narrow.at[0], upper, halo_send.at[1], halo_recv.at[1], preceding)
        down.start()
        up.start()
        own_b[...] = mm(corner_ref[...], border_narrow)

        def local(slot):
            return mm(diag[slot], narrow[slot]) + mm(border[slot], border_narrow)

        def behind(slot):
            return mm(coupling_t[slot - 1], narrow[slot - 1])

        def inner(slot, carry):
            applied[slot] = local(slot) + mm(coupling[slot], narrow[slot + 1]) + behind(slot)
            return carry

        lax.fori_loop(1, last, inner, 0)
        top = local(0) + mm(coupling[0], narrow[1])
        applied[last] = local(last) + behind(last)
        down.wait_recv()
        is_first = jnp.logical_and(me == 0, first)
        applied[0] = top + jnp.where(is_first, 0.0, lower[...].astype(F32))
        up.wait_recv()
        is_last = jnp.logical_and(me == count - 1, core == 1)
        ahead = jnp.where(is_last, 0.0, upper[...].astype(F32)).astype(BF16)
        applied[last] = applied[last] + mm(coupling[last], ahead)
        down.wait_send()
        up.wait_send()

    def rows_of(device):
        return pl.ds(pl.multiple_of(device * rows, rows), rows)

    def sum_border(numerators, denominators, final=False):
        swap = remote(
            part.at[other], pair_land, pair_send.at[0], pair_recv.at[0], sibling
        )
        swap.start()
        swap.wait_recv()
        reduced[...] = part[core] + pair_land[...]

        def scatter(step):
            return remote(
                reduced.at[rows_of(peer(step))],
                landing.at[step],
                send_b.at[step],
                recv_b.at[step],
                (peer(step), core),
            )

        def scatter_start(step, carry):
            scatter(step).start()
            return carry

        def scatter_wait(step, so_far):
            scatter(step).wait_recv()
            return so_far + landing[step]

        def scatter_drain(step, carry):
            scatter(step).wait_send()
            return carry

        def reduce_rows():
            lax.fori_loop(1, count, scatter_start, 0)
            message[:rows] = lax.fori_loop(1, count, scatter_wait, reduced[rows_of(me)])

        if final:
            pl.when(first)(reduce_rows)
        else:
            reduce_rows()
        mine = message[:rows]
        border_part = jnp.where(first, own_b[rows_of(me)] + mine, 0.0)
        against = resid_b[rows_of(me)] * border_part
        squares = border_part * border_part
        numerators = numerators + jnp.sum(against.reshape(rows // 8, 8, columns), axis=0)
        denominators = denominators + jnp.sum(squares.reshape(rows // 8, 8, columns), axis=0)
        tile_row = lax.broadcasted_iota(jnp.int32, (8, columns), 0)
        message[rows:] = jnp.where(
            tile_row == 0,
            jnp.sum(numerators, axis=0, keepdims=True),
            jnp.where(tile_row == 1, jnp.sum(denominators, axis=0, keepdims=True), 0.0),
        )

        def gather(step, slot):
            return remote(
                message.at[pl.ds(rows, 8)] if final else message,
                last_tiles.at[slot] if final else gathered.at[slot],
                send_c.at[step],
                recv_last.at[step] if final else recv_c.at[step],
                (peer(step), core),
            )

        def gather_start(step, carry):
            gather(step, me).start()
            return carry

        def gather_wait(step, carry):
            gather(step, source(step)).wait_recv()
            return carry

        lax.fori_loop(1, count, gather_start, 0)
        if final:
            last_tiles[me] = message[rows:]
        else:
            gathered[me] = message[...]
        lax.fori_loop(1, count, gather_wait, 0)

        def place(device, tiles):
            if final:
                return tiles + last_tiles[device]
            total[core, rows_of(device)] = gathered[device, :rows, :]
            return tiles + gathered[device, rows:, :]

        tiles = lax.fori_loop(0, count, place, jnp.zeros((8, columns), F32))
        total[core, border_rows:] = tiles

        def half_total(owner):
            ref = total.at[owner, pl.ds(border_rows, 8)] if final else total.at[owner]
            return remote(ref, ref, pair_send.at[1], pair_recv.at[1], sibling)

        back = half_total(core)
        back.start()
        landed = half_total(other)
        landed.wait_recv()
        back.wait_send()
        swap.wait_send()

        def drain(step, carry):
            gather(step, me).wait_send()
            return carry

        def drain_rows():
            lax.fori_loop(1, count, scatter_drain, 0)

        if final:
            pl.when(first)(drain_rows)
        else:
            drain_rows()
        lax.fori_loop(1, count, drain, 0)
        both = total[0, border_rows:] + total[1, border_rows:]
        return (jnp.sum(both[0:1]), jnp.sum(both[1:2]))

    zero_tile = jnp.zeros((8, columns), F32)

    loads[0].wait()
    swaps[0].wait_recv()

    def begin(slot):
        value = live(slot, joined(start_own[slot], start_land[slot]))
        sol[slot] = value
        narrow[slot] = value.astype(BF16)

    each_slot(begin)
    loads[1].wait()

    def turn_coupling(slot):
        coupling_t[slot] = coupling[slot].T

    each_slot(turn_coupling)
    loads[2].wait()

    def turn_border(slot):
        border_t[slot] = border[slot].T

    each_slot(turn_border)
    swaps[1].wait_recv()
    sol_b[...] = joined(start_border_ref[...], start_border_land[...])
    loads[3].wait()
    operate(sol_b[...].astype(BF16))
    loads[4].wait()
    loads[5].wait()
    swaps[2].wait_recv()
    swaps[3].wait_recv()
    part[...] = jnp.zeros_like(part)

    def to_border(slot, blockwise):
        pair = jnp.concatenate([narrow[slot], blockwise.astype(BF16)], 1)
        sums = mm(border_t[slot], pair)
        part[0] = part[0] + sums[:, :columns]
        part[1] = part[1] + sums[:, columns:]

    def first_residual(slot):
        value = live(slot, joined(rhs_own[slot], rhs_land[slot]) - applied[slot])
        resid[slot] = value
        to_border(slot, live(slot, mm(inverse[slot], value.astype(BF16))))

    each_slot(first_residual)
    resid_b[...] = joined(rhs_border_ref[...], rhs_border_land[...])
    sum_border(zero_tile, zero_tile)
    resid_b[...] = resid_b[...] - (own_b[...] + total[0, :border_rows])
    schur_sum[...] = total[1, :border_rows]

    step_size = None
    for iteration in range(ITERS):
        more = iteration < ITERS - 1
        update_b[...] = jnp.dot(
            schur_ref[...],
            resid_b[...] - schur_sum[...],
            precision=lax.Precision.HIGHEST,
            preferred_element_type=F32,
        )
        border_narrow = update_b[...].astype(BF16)

        def precondition(slot, step_size=step_size, border_narrow=border_narrow):
            if step_size is not None:
                sol[slot] = sol[slot] + step_size * update[slot]
                resid[slot] = resid[slot] - step_size * applied[slot]
            lifted = mm(border[slot], border_narrow).astype(BF16)
            both = mm(
                inverse[slot], jnp.concatenate([resid[slot].astype(BF16), lifted], 1)
            )
            value = live(slot, both[:, :columns] - both[:, columns:])
            update[slot] = value
            narrow[slot] = value.astype(BF16)

        each_slot(precondition)
        operate(border_narrow)
        part[...] = jnp.zeros_like(part)

        def products(slot, carry, more=more):
            numerators, denominators = carry
            value = live(slot, applied[slot])
            applied[slot] = value
            if more:
                to_border(slot, live(slot, mm(inverse[slot], value.astype(BF16))))
            else:
                part[0] = part[0] + mm(border_t[slot], narrow[slot])
            return (
                numerators + folded(resid[slot] * value),
                denominators + folded(value * value),
            )

        tiles = lax.fori_loop(0, slots, products, (zero_tile, zero_tile), unroll=True)
        numerator, denominator = sum_border(*tiles, final=not more)
        step_size = numerator / (denominator + 1e-06)
        sol_b[...] = sol_b[...] + step_size * update_b[...]
        if more:
            applied_b = own_b[...] + total[0, :border_rows]
            resid_b[...] = resid_b[...] - step_size * applied_b
            schur_sum[...] = schur_sum[...] - step_size * total[1, :border_rows]

    def finish(slot):
        value = sol[slot] + step_size * update[slot]
        turned = value.T
        left, right = (turned[:half], turned[half:])
        out_ref[core * slots + slot] = jnp.where(first, left, right)
        out_send[slot] = jnp.where(first, right, left)

    each_slot(finish)
    share = remote(out_send, out_land, swap_send.at[4], swap_recv.at[4], sibling)
    share.start()
    turned_b = sol_b[...].T
    out_border_ref[...] = jnp.where(first, turned_b[:half], turned_b[half:])
    for swap in swaps:
        swap.wait_send()
    share.wait_recv()

    def place_out(slot):
        out_ref[other * slots + slot] = out_land[slot]

    each_slot(place_out)
    share.wait_send()


def shards(
    rhs_blocks,
    rhs_border,
    start_blocks,
    start_border,
    diag_blocks,
    block_inverses,
    couplings,
    border_couplings,
    border_block,
    schur_inverse,
    row_counts,
):
    count = lax.axis_size("ord")
    slots = rhs_blocks.shape[0] // 2
    row_total, half = rhs_blocks.shape[1:]
    columns = 2 * half
    border_rows = rhs_border.shape[0]
    rows = border_rows // count
    vmem = pl.BlockSpec(memory_space=pltpu.VMEM)
    anywhere = pl.BlockSpec(memory_space=pl.ANY)
    square = pltpu.VMEM((slots, row_total, row_total), BF16)
    halves = pltpu.VMEM((slots, half, row_total), F32)
    border_half = pltpu.VMEM((half, border_rows), F32)
    state = pltpu.VMEM((slots, row_total, columns), F32)
    edge = pltpu.VMEM((row_total, columns), BF16)
    border_state = pltpu.VMEM((border_rows, columns), F32)
    sems = pltpu.SemaphoreType.DMA
    turned_blocks, turned_border = pl.pallas_call(
        functools.partial(kernel, count),
        out_shape=(
            jax.ShapeDtypeStruct((2 * slots, half, row_total), F32),
            jax.ShapeDtypeStruct((half, border_rows), F32),
        ),
        in_specs=[anywhere] * 6 + [vmem] * 4 + [pl.BlockSpec(memory_space=pltpu.SMEM)],
        out_specs=(vmem, vmem),
        scratch_shapes=[
            square,
            square,
            square,
            square,
            pltpu.VMEM((slots, row_total, border_rows), BF16),
            pltpu.VMEM((slots, border_rows, row_total), BF16),
            halves,
            halves,
            halves,
            halves,
            border_half,
            border_half,
            state,
            state,
            state,
            state,
            pltpu.VMEM((slots, row_total, columns), BF16),
            edge,
            edge,
            edge,
            border_state,
            border_state,
            border_state,
            border_state,
            border_state,
            pltpu.VMEM((2, border_rows, columns), F32),
            border_state,
            border_state,
            pltpu.VMEM((count, rows, columns), F32),
            pltpu.VMEM((rows + 8, columns), F32),
            pltpu.VMEM((count, rows + 8, columns), F32),
            pltpu.VMEM((count, 8, columns), F32),
            pltpu.VMEM((2, border_rows + 8, columns), F32),
            halves,
            halves,
            sems((6,)),
            sems((5,)),
            sems((5,)),
            sems((2,)),
            sems((2,)),
            sems((2,)),
            sems((2,)),
            sems((count,)),
            sems((count,)),
            sems((count,)),
            sems((count,)),
            sems((count,)),
        ],
        compiler_params=pltpu.CompilerParams(
            collective_id=0, has_side_effects=True, vmem_limit_bytes=58 * 2**20
        ),
        name="minimal_residual",
    )(
        jnp.swapaxes(rhs_blocks, 1, 2),
        jnp.swapaxes(start_blocks, 1, 2),
        diag_blocks,
        block_inverses,
        couplings,
        border_couplings,
        rhs_border.T,
        start_border.T,
        border_block,
        schur_inverse,
        row_counts,
    )
    return (jnp.swapaxes(turned_blocks, 1, 2), turned_border.T)


def solution(mesh):
    return jax.shard_map(
        shards,
        mesh=mesh,
        in_specs=(
            P("ord", None, "rhs"),
            P(None, "rhs"),
            P("ord", None, "rhs"),
            P(None, "rhs"),
            P("ord", None, None),
            P("ord", None, None),
            P("ord", None, None),
            P("ord", None, None),
            P(),
            P(),
            P("ord"),
        ),
        out_specs=(P("ord", None, "rhs"), P(None, "rhs")),
        check_vma=False,
    )
```
